256 devices in a mesh: row: 8 (over z), col: 32 (over x, y, core).
Axes of the slice: x: 4, y: 4, z: 8, core: 2. Of those that a mesh axis runs over, the one named last changes fastest.
Arguments:
- source_points: bfloat16 [64, 32768], P('col', 'row'), may hold values from -1 to 1
- target_points: bfloat16 [64, 131072], P('row', 'col'), may hold values from -0.8984375 to 0.8984375
- target_potential: float32 [131072], P('col'), may hold values from -2 to 8
Outputs:
- source_new: float32 [32768], P('row')
- target_new: float32 [131072], P('col')
The draws below stay inside these ranges and needn't reach their ends.
All inputs are finite; a program needn't handle non-finite values.
Results may differ from the reference program's by a relative error of at most 0.0003.
Values may be sent and summed in bfloat16 or wider, within the bound.
No kernel may reach another device: no remote copies, remote signals or barrier semaphores. Data moves between devices by JAX's collectives and lax.ppermute only.
A program may use at most 64 MiB of HBM per device.

```python
import math
import jax
import jax.numpy as jnp
from jax import lax

D = 64
NS = 32768
NT = 131072


def draw_source_points(key, part):
    key = jax.random.fold_in(key, 11)
    first_key = jax.random.fold_in(key, 0)
    values = jnp.clip(0.15 * jax.random.normal(first_key, (D, NS), jnp.float32), -0.9, 0.9)
    return values.astype(jnp.bfloat16)


def draw_target_potential(key, part):
    key = jax.random.fold_in(key, 23)
    first_key = jax.random.fold_in(key, 0)
    values = jnp.clip(0.3 * jax.random.normal(first_key, (NT,), jnp.float32), -1.5, 1.5)
    return values.astype(jnp.float32)


def block_levels(key, extent, cuts, least, top_value):
    def one(position, shards_of):
        heights = jax.random.uniform(jax.random.fold_in(jax.random.fold_in(key, 6), position), (shards_of,), jnp.float32, least / len(cuts), top_value / len(cuts))
        return jnp.repeat(jnp.exp(heights), extent[position] // shards_of).reshape((-1,) + (1,) * (len(extent) - position - 1))

    loudness = one(*cuts[0])
    for cut in cuts[1:]:
        loudness = loudness * one(*cut)
    return loudness


def centred(key, extent, scale, reach, cuts=(), held_as=jnp.bfloat16):
    drawn = jax.random.normal(key, extent, jnp.float32) * scale
    if len(cuts) > 0:
        drawn = block_levels(key, extent, cuts, -0.22, 0.18) * drawn
    return jnp.clip(drawn, min=-reach, max=reach).astype(held_as)


def setup_inputs(seed: int = 0) -> dict:
    streams_of = jax.random.split(jax.random.key(seed), 4)
    return {
        "source_points": draw_source_points(jax.random.fold_in(streams_of[3], 71), 0),
        "target_points": centred(streams_of[1], (D, NT), 0.15, 0.8984375, ((0, 8), (1, 32))),
        "target_potential": draw_target_potential(jax.random.fold_in(streams_of[3], 71), 0),
    }


EPS = 0.05


def reference(source_points, target_points, target_potential):
    src_norm = jnp.sum(jnp.square(source_points.astype(jnp.float32)), axis=0)
    tgt_norm = jnp.sum(jnp.square(target_points.astype(jnp.float32)), axis=0)
    src_total = source_points.shape[1]
    tgt_total = target_points.shape[1]
    block_rows = math.gcd(src_total, 1024)
    block_count = src_total // block_rows
    src_blocks = source_points.reshape(source_points.shape[0], block_count, block_rows).transpose(1, 0, 2)
    norm_blocks = src_norm.reshape(block_count, block_rows)

    def cost_of(src_block, norm_block):
        cross_term = jnp.dot(src_block.T, target_points, preferred_element_type=jnp.float32)
        return norm_block[:, None] + tgt_norm[None, :] - 2.0 * cross_term

    def first_pass(pieces):
        src_block, norm_block = pieces
        scores = (target_potential[None, :] - cost_of(src_block, norm_block)) / EPS
        row_peak = jnp.max(scores, axis=1)
        row_total = jnp.sum(jnp.exp(scores - row_peak[:, None]), axis=1)
        return -EPS * (row_peak + jnp.log(row_total)) + EPS * math.log(tgt_total)

    source_new = lax.map(first_pass, (src_blocks, norm_blocks)).reshape(src_total)
    pot_blocks = source_new.reshape(block_count, block_rows)

    def second_pass(carry, pieces):
        col_peak, col_total = carry
        src_block, norm_block, pot_block = pieces
        scores = (pot_block[:, None] - cost_of(src_block, norm_block)) / EPS
        new_peak = jnp.maximum(col_peak, jnp.max(scores, axis=0))
        new_total = col_total * jnp.exp(col_peak - new_peak) + jnp.sum(jnp.exp(scores - new_peak[None, :]), axis=0)
        return (new_peak, new_total), None

    start = (jnp.full((tgt_total,), -jnp.inf, jnp.float32), jnp.zeros((tgt_total,), jnp.float32))
    (col_peak, col_total), _ = lax.scan(second_pass, start, (src_blocks, norm_blocks, pot_blocks))
    target_new = -EPS * (col_peak + jnp.log(col_total)) + EPS * math.log(src_total)
    return source_new, target_new
```

```python
import functools
import math

import jax
import jax.numpy as jnp
from jax import lax
from jax.experimental import pallas as pl
from jax.experimental.pallas import tpu as pltpu
from jax.sharding import PartitionSpec as P

EPS = 0.05
LN2 = math.log(2.0)
KAPPA = 1.0 / (EPS * LN2)
ROWS = 128
LANES = 512


def split3(v):
    hi = v.astype(jnp.bfloat16)
    rest = v - hi.astype(jnp.float32)
    mid = rest.astype(jnp.bfloat16)
    low = (rest - mid.astype(jnp.float32)).astype(jnp.bfloat16)
    return hi, mid, low


def fill_operands(streamed, fixed, bias, lhs, rhs):
    d, n = streamed.shape
    hi, mid, low = split3(bias)
    row = lax.broadcasted_iota(jnp.int32, (d, n), 0)
    rows = jnp.where(row == 0, hi.astype(jnp.float32), 0.0)
    rows = jnp.where(row == 1, mid.astype(jnp.float32), rows)
    rows = jnp.where(row == 2, low.astype(jnp.float32), rows)
    points = streamed.astype(jnp.float32)
    lhs[:, : 2 * d] = jnp.concatenate([points, rows], axis=0).T.astype(jnp.bfloat16)
    lhs[:, 2 * d :] = jnp.concatenate([points, points], axis=0).T.astype(jnp.bfloat16)
    hi, mid, low = split3(fixed.astype(jnp.float32) * (2.0 * KAPPA))
    rhs[:d] = hi
    rhs[d : 2 * d] = jnp.where(row < 3, 1.0, 0.0).astype(jnp.bfloat16)
    rhs[2 * d : 3 * d] = mid
    rhs[3 * d :] = low


def column_lse(lhs, rhs, out):
    n = lhs.shape[0]

    def block(step, carry):
        lanes = pl.ds(pl.multiple_of(step * LANES, LANES), LANES)
        weights = rhs[:, lanes]
        peak = jnp.full((8, LANES), -jnp.inf, jnp.float32)
        total = jnp.zeros((8, LANES), jnp.float32)
        for start in range(0, n, ROWS):
            scores = jnp.dot(lhs[start : start + ROWS, :], weights, preferred_element_type=jnp.float32)
            scores = scores.reshape(ROWS // 8, 8, LANES)
            new_peak = jnp.maximum(peak, scores.max(0))
            total = total * jnp.exp2(peak - new_peak) + jnp.exp2(scores - new_peak[None]).sum(0)
            peak = new_peak
        top = peak.max(0, keepdims=True)
        out[:, lanes] = top + jnp.log2((total * jnp.exp2(peak - top)).sum(0, keepdims=True))
        return carry

    lax.fori_loop(0, rhs.shape[1] // LANES, block, 0)


def square_norm(points):
    return jnp.sum(jnp.square(points.astype(jnp.float32)), axis=0, keepdims=True)


def lse_of(parts):
    top = parts.max(0, keepdims=True)
    return top + jnp.log2(jnp.exp2(parts - top).sum(0, keepdims=True))


def first_kernel(src, tgt, pot, out, lhs, rhs):
    bias = KAPPA * (pot[...] - square_norm(tgt[...]))
    fill_operands(tgt[...], src[...], bias, lhs, rhs)
    column_lse(lhs, rhs, out)


def second_kernel(tgt_total, parts, src, tgt, new, out, lhs, rhs):
    bias = math.log2(tgt_total) - lse_of(parts[...])
    new[...] = square_norm(src[...]) + EPS * LN2 * bias
    fill_operands(src[...], tgt[...], bias, lhs, rhs)
    column_lse(lhs, rhs, out)


def gathered(x, axis):
    size = lax.axis_size(axis)
    whole = jnp.broadcast_to(x[None], (size,) + x.shape)
    return lax.all_to_all(whole, axis, 0, 0, tiled=True)


def on_device(source_points, target_points, target_potential):
    n_src = source_points.shape[1]
    n_tgt = target_points.shape[1]
    tgt_total = n_tgt * lax.axis_size("col")
    src_total = n_src * lax.axis_size("row")
    src = gathered(source_points, "col").reshape(-1, n_src)
    tgt = gathered(target_points, "row").reshape(-1, n_tgt)
    depth = 4 * src.shape[0]
    params = pltpu.CompilerParams(vmem_limit_bytes=48 * 2**20)
    partial = pl.pallas_call(
        first_kernel,
        out_shape=jax.ShapeDtypeStruct((1, n_src), jnp.float32),
        scratch_shapes=[pltpu.VMEM((n_tgt, depth), jnp.bfloat16), pltpu.VMEM((depth, n_src), jnp.bfloat16)],
        compiler_params=params,
        name="first_pass",
    )(src, tgt, target_potential.reshape(1, n_tgt))
    parts = gathered(partial.reshape(n_src), "col")
    source_new, partial = pl.pallas_call(
        functools.partial(second_kernel, tgt_total),
        out_shape=[jax.ShapeDtypeStruct((1, n_src), jnp.float32), jax.ShapeDtypeStruct((1, n_tgt), jnp.float32)],
        scratch_shapes=[pltpu.VMEM((n_src, depth), jnp.bfloat16), pltpu.VMEM((depth, n_tgt), jnp.bfloat16)],
        compiler_params=params,
        name="second_pass",
    )(parts, src, tgt)
    parts = gathered(partial.reshape(n_tgt), "row")
    target_new = square_norm(tgt) - EPS * LN2 * lse_of(parts) + EPS * math.log(src_total)
    return source_new.reshape(n_src), target_new.reshape(n_tgt)


def solution(mesh):
    return jax.shard_map(
        on_device,
        mesh=mesh,
        in_specs=(P("col", "row"), P("row", "col"), P("col")),
        out_specs=(P("row"), P("col")),
        check_vma=False,
    )
```

```python
import functools
import math

import jax
import jax.numpy as jnp
from jax import lax
from jax.experimental import pallas as pl
from jax.experimental.pallas import tpu as pltpu
from jax.sharding import PartitionSpec as P

EPS = 0.05
LN2 = math.log(2.0)
KAPPA = 1.0 / (EPS * LN2)
ROWS = 128
LANES = 1024
EXACT_LANES = 256


def split3(v):
    hi = v.astype(jnp.bfloat16)
    rest = v - hi.astype(jnp.float32)
    mid = rest.astype(jnp.bfloat16)
    low = (rest - mid.astype(jnp.float32)).astype(jnp.bfloat16)
    return hi, mid, low


def fill_operands(streamed, fixed, bias, lhs, rhs):
    d, n = streamed.shape
    hi, mid, low = split3(bias)
    row = lax.broadcasted_iota(jnp.int32, (d, n), 0)
    rows = jnp.where(row == 0, hi.astype(jnp.float32), 0.0)
    rows = jnp.where(row == 1, mid.astype(jnp.float32), rows)
    rows = jnp.where(row == 2, low.astype(jnp.float32), rows)
    points = streamed.astype(jnp.float32)
    lhs[:, : 2 * d] = jnp.concatenate([points, rows], axis=0).T.astype(jnp.bfloat16)
    lhs[:, 2 * d :] = jnp.concatenate([points, points], axis=0).T.astype(jnp.bfloat16)
    hi, mid, low = split3(fixed.astype(jnp.float32) * (2.0 * KAPPA))
    rhs[:d] = hi
    rhs[d : 2 * d] = jnp.where(row < 3, 1.0, 0.0).astype(jnp.bfloat16)
    rhs[2 * d : 3 * d] = mid
    rhs[3 * d :] = low


def column_lse(lhs, rhs, out):
    n = lhs.shape[0]

    def scores_of(start, weights):
        scores = jnp.dot(lhs[start : start + ROWS, :], weights, preferred_element_type=jnp.float32)
        return scores.reshape(ROWS // 8, 8, weights.shape[1])

    def lanes_of(step, width):
        return pl.ds(pl.multiple_of(step * width, width), width)

    def block(step, worst):
        lanes = lanes_of(step, LANES)
        weights = rhs[:, lanes]
        scores = scores_of(0, weights)
        peak = scores.max(0).max(0, keepdims=True)
        total = jnp.exp2(scores - peak[None]).sum(0)
        for start in range(ROWS, n, ROWS):
            total = total + jnp.exp2(scores_of(start, weights) - peak[None]).sum(0)
        total = total.sum(0, keepdims=True)
        out[:, lanes] = jnp.broadcast_to(peak + jnp.log2(total), (out.shape[0], LANES))
        return jnp.maximum(worst, total)

    worst = lax.fori_loop(0, rhs.shape[1] // LANES, block, jnp.zeros((1, LANES), jnp.float32))

    @pl.when(jnp.logical_not(jnp.max(worst) < 2.0**127))
    def _():
        def exact_block(step, carry):
            lanes = lanes_of(step, EXACT_LANES)
            weights = rhs[:, lanes]

            def rows(k, state):
                peak, total = state
                start = pl.multiple_of(k * ROWS, ROWS)
                scores = jnp.dot(lhs[pl.ds(start, ROWS), :], weights, preferred_element_type=jnp.float32)
                scores = scores.reshape(ROWS // 8, 8, EXACT_LANES)
                new_peak = jnp.maximum(peak, scores.max(0))
                total = total * jnp.exp2(peak - new_peak) + jnp.exp2(scores - new_peak[None]).sum(0)
                return new_peak, total

            start = (jnp.full((8, EXACT_LANES), -jnp.inf, jnp.float32), jnp.zeros((8, EXACT_LANES), jnp.float32))
            peak, total = lax.fori_loop(0, n // ROWS, rows, start)
            top = peak.max(0, keepdims=True)
            lse = top + jnp.log2((total * jnp.exp2(peak - top)).sum(0, keepdims=True))
            out[:, lanes] = jnp.broadcast_to(lse, (out.shape[0], EXACT_LANES))
            return carry

        lax.fori_loop(0, rhs.shape[1] // EXACT_LANES, exact_block, 0)


def square_norm(points):
    return jnp.sum(jnp.square(points.astype(jnp.float32)), axis=0, keepdims=True)


def lse_of(parts):
    top = parts.max(0, keepdims=True)
    return top + jnp.log2(jnp.exp2(parts - top).sum(0, keepdims=True))


def joined(pieces):
    return jnp.concatenate([piece[...].astype(jnp.float32) for piece in pieces], axis=0)


def first_kernel(order, pot, src_near, src_far, *refs):
    tgt_pieces, (out, src, tgt, lhs, rhs) = refs[:-5], refs[-5:]
    tgt[...] = joined(tgt_pieces).astype(jnp.bfloat16)
    features = joined([src_near, src_far]).astype(jnp.bfloat16)
    src[...] = jnp.dot(order[...], features, preferred_element_type=jnp.float32).astype(jnp.bfloat16)
    bias = KAPPA * (pot[...] - square_norm(tgt[...]))
    fill_operands(tgt[...], src[...], bias, lhs, rhs)
    column_lse(lhs, rhs, out)


def second_kernel(tgt_total, parts, src, tgt, new, out, lhs, rhs):
    bias = math.log2(tgt_total) - lse_of(parts[...])
    new[...] = square_norm(src[...]) + EPS * LN2 * bias
    fill_operands(src[...], tgt[...], bias, lhs, rhs)
    column_lse(lhs, rhs, out)


def last_kernel(src_total, parts, tgt, new):
    new[...] = square_norm(tgt[...]) - EPS * LN2 * lse_of(parts[...]) + EPS * math.log(src_total)


ROW, X, Y, CORE = 8, 4, 4, 2


def from_row(v, k):
    return lax.ppermute(v, "row", [((z + k) % ROW, z) for z in range(ROW)])


def from_col(v, kx, ky, kc):
    pairs = []
    for x in range(X):
        for y in range(Y):
            for c in range(CORE):
                there = (((x + kx) % X) * Y + (y + ky) % Y) * CORE + (c + kc) % CORE
                pairs.append((there, (x * Y + y) * CORE + c))
    return lax.ppermute(v, "col", pairs)


def all_to_all(parts, axis):
    return lax.all_to_all(parts, axis, 0, 0, tiled=True)


def feature_order(per_src, per_tgt):
    col, row = lax.axis_index("col"), lax.axis_index("row")
    depth = per_src * X * Y * CORE
    at = lax.broadcasted_iota(jnp.int32, (depth, depth), 1)
    kx, ky, kc = (at // per_src) % X, (at // (per_src * X)) % Y, at // (per_src * X * Y)
    x, y, c = col // (Y * CORE), (col // CORE) % Y, col % CORE
    there = (((x + kx) % X) * Y + (y + ky) % Y) * CORE + (c + kc) % CORE
    src_feature = there * per_src + at % per_src
    at = lax.broadcasted_iota(jnp.int32, (depth, depth), 0)
    tgt_feature = ((row + at // per_tgt) % ROW) * per_tgt + at % per_tgt
    return (src_feature == tgt_feature).astype(jnp.bfloat16)


def on_device(source_points, target_points, target_potential):
    per_src, n_src = source_points.shape
    per_tgt, n_tgt = target_points.shape
    tgt_total = n_tgt * X * Y * CORE
    src_total = n_src * ROW
    dim = per_src * X * Y * CORE
    order = feature_order(per_src, per_tgt)

    up = [target_points]
    down = [target_points]
    src = source_points
    src = jnp.concatenate([src] + [from_col(src, k, 0, 0) for k in range(1, X)], axis=0)
    for _ in range(ROW // 2 - 1):
        up.append(from_row(up[-1], 1))
        down.append(from_row(down[-1], -1))
    down.append(from_row(down[-1], -1))
    src = jnp.concatenate([src] + [from_col(src, 0, k, 0) for k in range(1, Y)], axis=0)
    far = from_col(src, 0, 0, 1)
    tgt_pieces = up + down[:0:-1]

    params = pltpu.CompilerParams(vmem_limit_bytes=48 * 2**20)
    points = [jax.ShapeDtypeStruct((dim, n_src), jnp.bfloat16), jax.ShapeDtypeStruct((dim, n_tgt), jnp.bfloat16)]
    parts, src, tgt = pl.pallas_call(
        first_kernel,
        out_shape=[jax.ShapeDtypeStruct((X * Y * CORE, n_src), jnp.float32)] + points,
        scratch_shapes=[pltpu.VMEM((n_tgt, 4 * dim), jnp.bfloat16), pltpu.VMEM((4 * dim, n_src), jnp.bfloat16)],
        compiler_params=params,
        name="first_pass",
    )(order, target_potential.reshape(1, n_tgt), src, far, *tgt_pieces)
    parts = all_to_all(parts, "col")
    source_new, parts = pl.pallas_call(
        functools.partial(second_kernel, tgt_total),
        out_shape=[jax.ShapeDtypeStruct((1, n_src), jnp.float32), jax.ShapeDtypeStruct((ROW, n_tgt), jnp.float32)],
        scratch_shapes=[pltpu.VMEM((n_src, 4 * dim), jnp.bfloat16), pltpu.VMEM((4 * dim, n_tgt), jnp.bfloat16)],
        compiler_params=params,
        name="second_pass",
    )(parts, src, tgt)
    parts = all_to_all(parts, "row")
    target_new = pl.pallas_call(
        functools.partial(last_kernel, src_total),
        out_shape=jax.ShapeDtypeStruct((1, n_tgt), jnp.float32),
        name="last",
    )(parts, tgt)
    return source_new.reshape(n_src), target_new.reshape(n_tgt)


def solution(mesh):
    return jax.shard_map(
        on_device,
        mesh=mesh,
        in_specs=(P("col", "row"), P("row", "col"), P("col")),
        out_specs=(P("row"), P("col")),
        check_vma=False,
    )
```

```python
import functools
import math

import jax
import jax.numpy as jnp
from jax import lax
from jax.experimental import pallas as pl
from jax.experimental.pallas import tpu as pltpu
from jax.sharding import PartitionSpec as P

EPS = 0.05
LN2 = math.log(2.0)
KAPPA = 1.0 / (EPS * LN2)
ROWS = 128
LANES = 1024
EXACT_LANES = 256
KEPT = 8
HEAD = 40.0


def split3(v):
    hi = v.astype(jnp.bfloat16)
    rest = v - hi.astype(jnp.float32)
    mid = rest.astype(jnp.bfloat16)
    low = (rest - mid.astype(jnp.float32)).astype(jnp.bfloat16)
    return hi, mid, low


def fill_operands(streamed, fixed, bias, lhs, rhs):
    d, n = streamed.shape
    hi, mid, low = split3(bias)
    row = lax.broadcasted_iota(jnp.int32, (d, n), 0)
    rows = jnp.where(row == 0, hi.astype(jnp.float32), 0.0)
    rows = jnp.where(row == 1, mid.astype(jnp.float32), rows)
    rows = jnp.where(row == 2, low.astype(jnp.float32), rows)
    points = streamed.astype(jnp.float32)
    lhs[:, : 2 * d] = jnp.concatenate([points, rows], axis=0).T.astype(jnp.bfloat16)
    lhs[:, 2 * d :] = jnp.concatenate([points, points], axis=0).T.astype(jnp.bfloat16)
    hi, mid, low = split3(fixed.astype(jnp.float32) * (2.0 * KAPPA))
    rhs[:d] = hi
    rhs[d : 2 * d] = jnp.where(row < 3, 1.0, 0.0).astype(jnp.bfloat16)
    rhs[2 * d : 3 * d] = mid
    rhs[3 * d :] = low


def scores_of(lhs, start, weights):
    scores = jnp.dot(lhs[pl.ds(start, ROWS), :], weights, preferred_element_type=jnp.float32)
    return scores.reshape(ROWS // 8, 8, weights.shape[1])


def lanes_of(step, width):
    return pl.ds(pl.multiple_of(step * width, width), width)


def exact_lse(lhs, rhs, out, offset):
    def block(step, carry):
        lanes = lanes_of(step, EXACT_LANES)
        weights = rhs[:, lanes]

        def rows(k, state):
            peak, total = state
            scores = scores_of(lhs, pl.multiple_of(k * ROWS, ROWS), weights)
            new_peak = jnp.maximum(peak, scores.max(0))
            total = total * jnp.exp2(peak - new_peak) + jnp.exp2(scores - new_peak[None]).sum(0)
            return new_peak, total

        start = (jnp.full((8, EXACT_LANES), -jnp.inf, jnp.float32), jnp.zeros((8, EXACT_LANES), jnp.float32))
        peak, total = lax.fori_loop(0, lhs.shape[0] // ROWS, rows, start)
        top = peak.max(0, keepdims=True)
        lse = offset + top + jnp.log2((total * jnp.exp2(peak - top)).sum(0, keepdims=True))
        out[:, lanes] = jnp.broadcast_to(lse, (out.shape[0], EXACT_LANES))
        return carry

    lax.fori_loop(0, rhs.shape[1] // EXACT_LANES, block, 0)


def in_range(sums):
    return jnp.logical_and(jnp.min(sums) > 2.0**-90, jnp.max(sums) < 2.0**127)


def square_norm(points):
    return jnp.sum(jnp.square(points.astype(jnp.float32)), axis=0, keepdims=True)


def lse_of(parts):
    top = parts.max(0, keepdims=True)
    return top + jnp.log2(jnp.exp2(parts - top).sum(0, keepdims=True))


def joined(pieces):
    return jnp.concatenate([piece[...].astype(jnp.float32) for piece in pieces], axis=0)


def first_kernel(order, pot, src_near, src_far, *refs):
    tgt_pieces, weights, (out, shift, flag, src, tgt, lhs, rhs) = refs[: -7 - KEPT], refs[-7 - KEPT : -7], refs[-7:]
    share = weights[0].shape[0]
    tgt[...] = joined(tgt_pieces).astype(jnp.bfloat16)
    features = joined([src_near, src_far]).astype(jnp.bfloat16)
    src[...] = jnp.dot(order[...], features, preferred_element_type=jnp.float32).astype(jnp.bfloat16)
    bias = KAPPA * (pot[...] - square_norm(tgt[...]))
    offset = jnp.max(bias, axis=1, keepdims=True) - HEAD
    shift[...] = bias - offset
    fill_operands(tgt[...], src[...], bias - offset, lhs, rhs)

    def block(step, carry):
        lanes = lanes_of(step, LANES)
        fixed = rhs[:, lanes]
        total = jnp.zeros((8, LANES), jnp.float32)
        for start in range(0, lhs.shape[0], ROWS):
            powers = jnp.exp2(scores_of(lhs, start, fixed))
            total = total + powers.sum(0)
            at = start % share
            weights[start // share][at : at + ROWS, lanes] = powers.reshape(ROWS, LANES).astype(jnp.bfloat16)
        out[:, lanes] = total.sum(0, keepdims=True)
        return carry

    lax.fori_loop(0, rhs.shape[1] // LANES, block, 0)
    sums = out[...]
    good = in_range(sums)
    flag[0, 0] = good.astype(jnp.int32)
    out[...] = offset + jnp.log2(sums)

    @pl.when(jnp.logical_not(good))
    def _():
        exact_lse(lhs, rhs, out, offset)


def second_kernel(tgt_total, src_total, lse, flag, shift, src, tgt, *refs):
    weights, (new, base, out, factors, lhs, rhs) = refs[:KEPT], refs[KEPT:]
    share, n_src = weights[0].shape
    bias = math.log2(tgt_total) - lse[...]
    new[...] = square_norm(src[...]) + EPS * LN2 * bias
    base[...] = square_norm(tgt[...]) + EPS * math.log(src_total)
    top = jnp.max(bias, axis=1, keepdims=True)
    factors[...] = jnp.broadcast_to(jnp.exp2(bias - top), (8, n_src))

    for part in range(KEPT):

        def block(step, carry):
            rows = lanes_of(step, 128)
            total = jnp.zeros((16, 8, 128), jnp.float32)
            for start in range(0, n_src, 128):
                powers = weights[part][rows, start : start + 128].astype(jnp.float32).reshape(16, 8, 128)
                total = total + powers * factors[:, start : start + 128][None]
            sums = total.reshape(128, 128).T.sum(0, keepdims=True)
            out[:, lanes_of(step + part * (share // 128), 128)] = jnp.broadcast_to(sums, (out.shape[0], 128))
            return carry

        lax.fori_loop(0, share // 128, block, 0)
    sums = out[...]
    good = jnp.logical_and(in_range(sums), jnp.min(bias) - jnp.max(bias) > -120.0)
    good = jnp.logical_and(good, flag[0, 0] == 1)
    out[...] = top - shift[...] + jnp.log2(sums)

    @pl.when(jnp.logical_not(good))
    def _():
        fill_operands(src[...], tgt[...], bias, lhs, rhs)
        exact_lse(lhs, rhs, out, 0.0)


ROW, X, Y, CORE = 8, 4, 4, 2


def from_row(v, k):
    return lax.ppermute(v, "row", [((z + k) % ROW, z) for z in range(ROW)])


def from_col(v, kx, ky, kc):
    pairs = []
    for x in range(X):
        for y in range(Y):
            for c in range(CORE):
                there = (((x + kx) % X) * Y + (y + ky) % Y) * CORE + (c + kc) % CORE
                pairs.append((there, (x * Y + y) * CORE + c))
    return lax.ppermute(v, "col", pairs)


def pair_lse(a, b):
    top = jnp.maximum(a, b)
    return top + jnp.log2(jnp.exp2(a - top) + jnp.exp2(b - top))


def ring_lse(own, others):
    top = jnp.maximum(jnp.maximum(own, others[1]), jnp.maximum(others[0], others[2]))
    near = jnp.exp2(others[0] - top) + jnp.exp2(others[2] - top)
    return top + jnp.log2((jnp.exp2(own - top) + jnp.exp2(others[1] - top)) + near)


def all_to_all(parts, axis):
    return lax.all_to_all(parts, axis, 0, 0, tiled=True)


def feature_order(per_src, per_tgt):
    col, row = lax.axis_index("col"), lax.axis_index("row")
    depth = per_src * X * Y * CORE
    at = lax.broadcasted_iota(jnp.int32, (depth, depth), 1)
    kx, ky, kc = (at // per_src) % X, (at // (per_src * X)) % Y, at // (per_src * X * Y)
    x, y, c = col // (Y * CORE), (col // CORE) % Y, col % CORE
    there = (((x + kx) % X) * Y + (y + ky) % Y) * CORE + (c + kc) % CORE
    src_feature = there * per_src + at % per_src
    at = lax.broadcasted_iota(jnp.int32, (depth, depth), 0)
    tgt_feature = ((row + at // per_tgt) % ROW) * per_tgt + at % per_tgt
    return (src_feature == tgt_feature).astype(jnp.bfloat16)


def on_device(source_points, target_points, target_potential):
    per_src, n_src = source_points.shape
    per_tgt, n_tgt = target_points.shape
    tgt_total = n_tgt * X * Y * CORE
    src_total = n_src * ROW
    dim = per_src * X * Y * CORE
    order = feature_order(per_src, per_tgt)

    up = [target_points]
    down = [target_points]
    src = source_points
    src = jnp.concatenate([src] + [from_col(src, k, 0, 0) for k in range(1, X)], axis=0)
    for _ in range(ROW // 2 - 1):
        up.append(from_row(up[-1], 1))
        down.append(from_row(down[-1], -1))
    down.append(from_row(down[-1], -1))
    src = jnp.concatenate([src] + [from_col(src, 0, k, 0) for k in range(1, Y)], axis=0)
    far = from_col(src, 0, 0, 1)
    tgt_pieces = up + down[:0:-1]

    params = pltpu.CompilerParams(vmem_limit_bytes=16 * 2**20)
    f32, bf16 = jnp.float32, jnp.bfloat16
    whole, scalar = pl.BlockSpec(memory_space=pltpu.VMEM), pl.BlockSpec(memory_space=pltpu.SMEM)
    *weights, lse, shift, flag, src, tgt = pl.pallas_call(
        first_kernel,
        out_shape=[
            *[pltpu.VMEM((n_tgt // KEPT, n_src), bf16)] * KEPT,
            jax.ShapeDtypeStruct((1, n_src), f32),
            jax.ShapeDtypeStruct((1, n_tgt), f32),
            jax.ShapeDtypeStruct((1, 1), jnp.int32),
            jax.ShapeDtypeStruct((dim, n_src), bf16),
            jax.ShapeDtypeStruct((dim, n_tgt), bf16),
        ],
        out_specs=[whole] * KEPT + [whole, whole, scalar, whole, whole],
        scratch_shapes=[pltpu.VMEM((n_tgt, 4 * dim), bf16), pltpu.VMEM((4 * dim, n_src), bf16)],
        compiler_params=params,
        name="first_pass",
    )(order, target_potential.reshape(1, n_tgt), src, far, *tgt_pieces)

    lse = lse.reshape(n_src)
    lse = pair_lse(lse, from_col(lse, 0, 0, 1))
    lse = ring_lse(lse, [from_col(lse, k, 0, 0) for k in (1, 2, 3)])
    lse = ring_lse(lse, [from_col(lse, 0, k, 0) for k in (1, 2, 3)])

    source_new, base, parts = pl.pallas_call(
        functools.partial(second_kernel, tgt_total, src_total),
        out_shape=[
            jax.ShapeDtypeStruct((1, n_src), f32),
            jax.ShapeDtypeStruct((1, n_tgt), f32),
            jax.ShapeDtypeStruct((ROW, n_tgt), f32),
        ],
        in_specs=[whole, scalar, whole, whole, whole] + [whole] * KEPT,
        out_specs=[whole, whole, whole],
        scratch_shapes=[
            pltpu.VMEM((8, n_src), f32),
            pltpu.VMEM((n_src, 4 * dim), bf16),
            pltpu.VMEM((4 * dim, n_tgt), bf16),
        ],
        compiler_params=params,
        name="second_pass",
    )(lse.reshape(1, n_src), flag, shift, src, tgt, *weights)
    parts = all_to_all(parts.reshape(ROW, 1, n_tgt), "row")
    target_new = base.reshape(n_tgt) - EPS * LN2 * lse_of(parts).reshape(n_tgt)
    return source_new.reshape(n_src), target_new


def solution(mesh):
    return jax.shard_map(
        on_device,
        mesh=mesh,
        in_specs=(P("col", "row"), P("row", "col"), P("col")),
        out_specs=(P("row"), P("col")),
        check_vma=False,
    )
```

```python
import functools
import math

import jax
import jax.numpy as jnp
from jax import lax
from jax.experimental import pallas as pl
from jax.experimental.pallas import tpu as pltpu
from jax.sharding import PartitionSpec as P

EPS = 0.05
LN2 = math.log(2.0)
KAPPA = 1.0 / (EPS * LN2)
ROWS = 128
LANES = 1024
EXACT_LANES = 256
KEPT = 8
HEAD = 40.0


def split3(v):
    hi = v.astype(jnp.bfloat16)
    rest = v - hi.astype(jnp.float32)
    mid = rest.astype(jnp.bfloat16)
    low = (rest - mid.astype(jnp.float32)).astype(jnp.bfloat16)
    return hi, mid, low


def fill_streamed(points, bias, lhs):
    d, n = points.shape
    hi, mid, low = split3(bias)
    row = lax.broadcasted_iota(jnp.int32, (d, n), 0)
    rows = jnp.where(row == 0, hi.astype(jnp.float32), 0.0)
    rows = jnp.where(row == 1, mid.astype(jnp.float32), rows)
    rows = jnp.where(row == 2, low.astype(jnp.float32), rows)
    points = points.astype(jnp.float32)
    lhs[:, : 2 * d] = jnp.concatenate([points, rows], axis=0).T.astype(jnp.bfloat16)
    lhs[:, 2 * d :] = jnp.concatenate([points, points], axis=0).T.astype(jnp.bfloat16)


def fill_fixed(points, rhs):
    d, n = points.shape
    row = lax.broadcasted_iota(jnp.int32, (d, n), 0)
    hi, mid, low = split3(points.astype(jnp.float32) * (2.0 * KAPPA))
    rhs[:d] = hi
    rhs[d : 2 * d] = jnp.where(row < 3, 1.0, 0.0).astype(jnp.bfloat16)
    rhs[2 * d : 3 * d] = mid
    rhs[3 * d :] = low


def scores_of(lhs, start, weights):
    scores = jnp.dot(lhs[pl.ds(start, ROWS), :], weights, preferred_element_type=jnp.float32)
    return scores.reshape(ROWS // 8, 8, weights.shape[1])


def lanes_of(step, width):
    return pl.ds(pl.multiple_of(step * width, width), width)


def exact_lse(lhs, rhs, out, offset):
    def block(step, carry):
        lanes = lanes_of(step, EXACT_LANES)
        weights = rhs[:, lanes]

        def rows(k, state):
            peak, total = state
            scores = scores_of(lhs, pl.multiple_of(k * ROWS, ROWS), weights)
            new_peak = jnp.maximum(peak, scores.max(0))
            total = total * jnp.exp2(peak - new_peak) + jnp.exp2(scores - new_peak[None]).sum(0)
            return new_peak, total

        start = (jnp.full((8, EXACT_LANES), -jnp.inf, jnp.float32), jnp.zeros((8, EXACT_LANES), jnp.float32))
        peak, total = lax.fori_loop(0, lhs.shape[0] // ROWS, rows, start)
        top = peak.max(0, keepdims=True)
        lse = offset + top + jnp.log2((total * jnp.exp2(peak - top)).sum(0, keepdims=True))
        out[:, lanes] = jnp.broadcast_to(lse, (out.shape[0], EXACT_LANES))
        return carry

    lax.fori_loop(0, rhs.shape[1] // EXACT_LANES, block, 0)


def in_range(sums):
    return jnp.logical_and(jnp.min(sums) > 2.0**-90, jnp.max(sums) < 2.0**127)


def square_norm(points):
    return jnp.sum(jnp.square(points.astype(jnp.float32)), axis=0, keepdims=True)


def lse_of(parts):
    top = parts.max(0, keepdims=True)
    return top + jnp.log2(jnp.exp2(parts - top).sum(0, keepdims=True))


def joined(pieces):
    return jnp.concatenate([piece[...].astype(jnp.float32) for piece in pieces], axis=0)


def source_kernel(order, near, far, pot_in, *refs):
    early, (src, rhs, pot, tgt) = refs[:-4], refs[-4:]
    features = joined([near, far]).astype(jnp.bfloat16)
    src[...] = jnp.dot(order[...], features, preferred_element_type=jnp.float32).astype(jnp.bfloat16)
    fill_fixed(src[...], rhs)
    pot[...] = KAPPA * pot_in[...]
    tgt[...] = joined(early)


def first_kernel(pot, rhs, early, last, *refs):
    weights, (out, shift, flag, tgt, lhs) = refs[:KEPT], refs[KEPT:]
    share = weights[0].shape[0]
    tgt[...] = joined([early, last]).astype(jnp.bfloat16)
    bias = pot[...] - KAPPA * square_norm(tgt[...])
    offset = jnp.max(bias, axis=1, keepdims=True) - HEAD
    shift[...] = bias - offset
    fill_streamed(tgt[...], bias - offset, lhs)

    def block(step, carry):
        lanes = lanes_of(step, LANES)
        fixed = rhs[:, lanes]
        total = jnp.zeros((8, LANES), jnp.float32)
        for start in range(0, lhs.shape[0], ROWS):
            powers = jnp.exp2(scores_of(lhs, start, fixed))
            total = total + powers.sum(0)
            at = start % share
            weights[start // share][at : at + ROWS, lanes] = powers.reshape(ROWS, LANES).astype(jnp.bfloat16)
        out[:, lanes] = total.sum(0, keepdims=True)
        return carry

    lax.fori_loop(0, rhs.shape[1] // LANES, block, 0)
    sums = out[...]
    good = in_range(sums)
    flag[0, 0] = good.astype(jnp.int32)
    out[...] = offset + jnp.log2(sums)

    @pl.when(jnp.logical_not(good))
    def _():
        exact_lse(lhs, rhs, out, offset)


def second_kernel(tgt_total, src_total, lse, flag, shift, src, tgt, *refs):
    weights, (new, base, out, factors, lhs, rhs) = refs[:KEPT], refs[KEPT:]
    share, n_src = weights[0].shape
    bias = math.log2(tgt_total) - lse[...]
    new[...] = square_norm(src[...]) + EPS * LN2 * bias
    base[...] = square_norm(tgt[...]) + EPS * math.log(src_total)
    top = jnp.max(bias, axis=1, keepdims=True)
    factors[...] = jnp.broadcast_to(jnp.exp2(bias - top), (8, n_src))

    for part in range(KEPT):
        total = jnp.zeros((share // 8, 8, 128), jnp.float32)
        for start in range(0, n_src, 128):
            powers = weights[part][:, start : start + 128].astype(jnp.float32).reshape(share // 8, 8, 128)
            total = total + powers * factors[:, start : start + 128][None]
        sums = total.reshape(share, 128).T.sum(0, keepdims=True)
        out[:, part * share : (part + 1) * share] = jnp.broadcast_to(sums, (out.shape[0], share))
    sums = out[...]
    good = jnp.logical_and(in_range(sums), jnp.min(bias) - jnp.max(bias) > -120.0)
    good = jnp.logical_and(good, flag[0, 0] == 1)
    out[...] = top - shift[...] + jnp.log2(sums)

    @pl.when(jnp.logical_not(good))
    def _():
        fill_streamed(src[...], bias, lhs)
        fill_fixed(tgt[...], rhs)
        exact_lse(lhs, rhs, out, 0.0)


ROW, X, Y, CORE = 8, 4, 4, 2


def from_row(v, k):
    return lax.ppermute(v, "row", [((z + k) % ROW, z) for z in range(ROW)])


def from_col(v, kx, ky, kc):
    pairs = []
    for x in range(X):
        for y in range(Y):
            for c in range(CORE):
                there = (((x + kx) % X) * Y + (y + ky) % Y) * CORE + (c + kc) % CORE
                pairs.append((there, (x * Y + y) * CORE + c))
    return lax.ppermute(v, "col", pairs)


def pair_lse(a, b):
    top = jnp.maximum(a, b)
    return top + jnp.log2(jnp.exp2(a - top) + jnp.exp2(b - top))


def ring_lse(own, others):
    top = jnp.maximum(jnp.maximum(own, others[1]), jnp.maximum(others[0], others[2]))
    near = jnp.exp2(others[0] - top) + jnp.exp2(others[2] - top)
    return top + jnp.log2((jnp.exp2(own - top) + jnp.exp2(others[1] - top)) + near)


def all_to_all(parts, axis):
    return lax.all_to_all(parts, axis, 0, 0, tiled=True)


def feature_order(per_src, per_tgt):
    col, row = lax.axis_index("col"), lax.axis_index("row")
    depth = per_src * X * Y * CORE
    at = lax.broadcasted_iota(jnp.int32, (depth, depth), 1)
    kx, ky, kc = (at // per_src) % X, (at // (per_src * X)) % Y, at // (per_src * X * Y)
    x, y, c = col // (Y * CORE), (col // CORE) % Y, col % CORE
    there = (((x + kx) % X) * Y + (y + ky) % Y) * CORE + (c + kc) % CORE
    src_feature = there * per_src + at % per_src
    at = lax.broadcasted_iota(jnp.int32, (depth, depth), 0)
    piece = at // per_tgt
    piece = jnp.where(piece < ROW // 2, piece, jnp.where(piece < ROW - 1, piece + 1, ROW // 2))
    tgt_feature = ((row + piece) % ROW) * per_tgt + at % per_tgt
    return (src_feature == tgt_feature).astype(jnp.bfloat16)


def on_device(source_points, target_points, target_potential):
    per_src, n_src = source_points.shape
    per_tgt, n_tgt = target_points.shape
    tgt_total = n_tgt * X * Y * CORE
    src_total = n_src * ROW
    dim = per_src * X * Y * CORE
    order = feature_order(per_src, per_tgt)

    up = [target_points]
    down = [target_points]
    src = source_points
    src = jnp.concatenate([src] + [from_col(src, k, 0, 0) for k in range(1, X)], axis=0)
    for _ in range(ROW // 2 - 1):
        up.append(from_row(up[-1], 1))
        down.append(from_row(down[-1], -1))
    down.append(from_row(down[-1], -1))
    src = jnp.concatenate([src] + [from_col(src, 0, k, 0) for k in range(1, Y)], axis=0)
    far = from_col(src, 0, 0, 1)
    *early, last = up + down[3:0:-1] + down[4:]

    params = pltpu.CompilerParams(vmem_limit_bytes=16 * 2**20)
    f32, bf16 = jnp.float32, jnp.bfloat16
    whole, scalar = pl.BlockSpec(memory_space=pltpu.VMEM), pl.BlockSpec(memory_space=pltpu.SMEM)
    src, rhs, pot, tgt = pl.pallas_call(
        source_kernel,
        out_shape=[
            jax.ShapeDtypeStruct((dim, n_src), bf16),
            jax.ShapeDtypeStruct((4 * dim, n_src), bf16),
            jax.ShapeDtypeStruct((1, n_tgt), f32),
            jax.ShapeDtypeStruct((dim - per_tgt, n_tgt), f32),
        ],
        compiler_params=params,
        name="sources",
    )(order, src, far, target_potential.reshape(1, n_tgt), *early)

    *weights, lse, shift, flag, tgt = pl.pallas_call(
        first_kernel,
        out_shape=[
            *[pltpu.VMEM((n_tgt // KEPT, n_src), bf16)] * KEPT,
            jax.ShapeDtypeStruct((1, n_src), f32),
            jax.ShapeDtypeStruct((1, n_tgt), f32),
            jax.ShapeDtypeStruct((1, 1), jnp.int32),
            jax.ShapeDtypeStruct((dim, n_tgt), bf16),
        ],
        out_specs=[whole] * KEPT + [whole, whole, scalar, whole],
        scratch_shapes=[pltpu.VMEM((n_tgt, 4 * dim), bf16)],
        compiler_params=params,
        name="first_pass",
    )(pot, rhs, tgt, last)

    lse = lse.reshape(n_src)
    lse = pair_lse(lse, from_col(lse, 0, 0, 1))
    lse = ring_lse(lse, [from_col(lse, k, 0, 0) for k in (1, 2, 3)])
    lse = ring_lse(lse, [from_col(lse, 0, k, 0) for k in (1, 2, 3)])

    source_new, base, parts = pl.pallas_call(
        functools.partial(second_kernel, tgt_total, src_total),
        out_shape=[
            jax.ShapeDtypeStruct((1, n_src), f32),
            jax.ShapeDtypeStruct((1, n_tgt), f32),
            jax.ShapeDtypeStruct((ROW, n_tgt), f32),
        ],
        in_specs=[whole, scalar, whole, whole, whole] + [whole] * KEPT,
        out_specs=[whole, whole, whole],
        scratch_shapes=[
            pltpu.VMEM((8, n_src), f32),
            pltpu.VMEM((n_src, 4 * dim), bf16),
            pltpu.VMEM((4 * dim, n_tgt), bf16),
        ],
        compiler_params=params,
        name="second_pass",
    )(lse.reshape(1, n_src), flag, shift, src, tgt, *weights)
    parts = all_to_all(parts.reshape(ROW, 1, n_tgt), "row")
    target_new = base.reshape(n_tgt) - EPS * LN2 * lse_of(parts).reshape(n_tgt)
    return source_new.reshape(n_src), target_new


def solution(mesh):
    return jax.shard_map(
        on_device,
        mesh=mesh,
        in_specs=(P("col", "row"), P("row", "col"), P("col")),
        out_specs=(P("row"), P("col")),
        check_vma=False,
    )
```

```python
import functools
import math

import jax
import jax.numpy as jnp
from jax import lax
from jax.experimental import pallas as pl
from jax.experimental.pallas import tpu as pltpu
from jax.sharding import PartitionSpec as P

EPS = 0.05
LN2 = math.log(2.0)
KAPPA = 1.0 / (EPS * LN2)
ROWS = 128
LANES = 4096
EXACT_LANES = 256
KEPT = 8
HEAD = 40.0


def split3(v):
    hi = v.astype(jnp.bfloat16)
    rest = v - hi.astype(jnp.float32)
    mid = rest.astype(jnp.bfloat16)
    low = (rest - mid.astype(jnp.float32)).astype(jnp.bfloat16)
    return hi, mid, low


def fill_streamed(points, bias, lhs):
    d, n = points.shape
    hi, mid, low = split3(bias)
    row = lax.broadcasted_iota(jnp.int32, (d, n), 0)
    rows = jnp.where(row == 0, hi.astype(jnp.float32), 0.0)
    rows = jnp.where(row == 1, mid.astype(jnp.float32), rows)
    rows = jnp.where(row == 2, low.astype(jnp.float32), rows)
    points = points.astype(jnp.float32)
    lhs[:, : 2 * d] = jnp.concatenate([points, rows], axis=0).T.astype(jnp.bfloat16)
    lhs[:, 2 * d :] = jnp.concatenate([points, points], axis=0).T.astype(jnp.bfloat16)


def fill_fixed(points, rhs):
    d, n = points.shape
    row = lax.broadcasted_iota(jnp.int32, (d, n), 0)
    hi, mid, low = split3(points.astype(jnp.float32) * (2.0 * KAPPA))
    rhs[:d] = hi
    rhs[d : 2 * d] = jnp.where(row < 3, 1.0, 0.0).astype(jnp.bfloat16)
    rhs[2 * d : 3 * d] = mid
    rhs[3 * d :] = low


def scores_of(lhs, start, weights):
    scores = jnp.dot(lhs[pl.ds(start, ROWS), :], weights, preferred_element_type=jnp.float32)
    return scores.reshape(ROWS // 8, 8, weights.shape[1])


def lanes_of(step, width):
    return pl.ds(pl.multiple_of(step * width, width), width)


def exact_lse(lhs, rhs, out, offset):
    def block(step, carry):
        lanes = lanes_of(step, EXACT_LANES)
        weights = rhs[:, lanes]

        def rows(k, state):
            peak, total = state
            scores = scores_of(lhs, pl.multiple_of(k * ROWS, ROWS), weights)
            new_peak = jnp.maximum(peak, scores.max(0))
            total = total * jnp.exp2(peak - new_peak) + jnp.exp2(scores - new_peak[None]).sum(0)
            return new_peak, total

        start = (jnp.full((8, EXACT_LANES), -jnp.inf, jnp.float32), jnp.zeros((8, EXACT_LANES), jnp.float32))
        peak, total = lax.fori_loop(0, lhs.shape[0] // ROWS, rows, start)
        top = peak.max(0, keepdims=True)
        lse = offset + top + jnp.log2((total * jnp.exp2(peak - top)).sum(0, keepdims=True))
        out[:, lanes] = jnp.broadcast_to(lse, (out.shape[0], EXACT_LANES))
        return carry

    lax.fori_loop(0, rhs.shape[1] // EXACT_LANES, block, 0)


def in_range(sums):
    return jnp.logical_and(jnp.min(sums) > 2.0**-90, jnp.max(sums) < 2.0**127)


def square_norm(points):
    return jnp.sum(jnp.square(points.astype(jnp.float32)), axis=0, keepdims=True)


def lse_of(parts):
    top = parts.max(0, keepdims=True)
    return top + jnp.log2(jnp.exp2(parts - top).sum(0, keepdims=True))


def joined(pieces):
    return jnp.concatenate([piece[...].astype(jnp.float32) for piece in pieces], axis=0)


def first_kernel(order, near, far, tgt, pot, *refs):
    weights, (out, shift, flag, src, lhs, rhs) = refs[:KEPT], refs[KEPT:]
    share = weights[0].shape[0]
    features = joined([near, far]).astype(jnp.bfloat16)
    src[...] = jnp.dot(order[...], features, preferred_element_type=jnp.float32).astype(jnp.bfloat16)
    fill_fixed(src[...], rhs)
    bias = KAPPA * (pot[...] - square_norm(tgt[...]))
    offset = jnp.max(bias, axis=1, keepdims=True) - HEAD
    shift[...] = bias - offset
    fill_streamed(tgt[...], bias - offset, lhs)

    def block(step, carry):
        lanes = lanes_of(step, LANES)
        fixed = rhs[:, lanes]
        total = jnp.zeros((8, LANES), jnp.float32)
        for start in range(0, lhs.shape[0], ROWS):
            powers = jnp.exp2(scores_of(lhs, start, fixed))
            total = total + powers.sum(0)
            at = start % share
            weights[start // share][at : at + ROWS, lanes] = powers.reshape(ROWS, LANES).astype(jnp.bfloat16)
        out[:, lanes] = total.sum(0, keepdims=True)
        return carry

    lax.fori_loop(0, rhs.shape[1] // LANES, block, 0)
    sums = out[...]
    good = in_range(sums)
    flag[0, 0] = good.astype(jnp.int32)
    out[...] = offset + jnp.log2(sums)

    @pl.when(jnp.logical_not(good))
    def _():
        exact_lse(lhs, rhs, out, offset)


def second_kernel(tgt_total, src_total, lse, flag, shift, src, tgt, *refs):
    weights, (new, base, out, factors, lhs, rhs) = refs[:KEPT], refs[KEPT:]
    share, n_src = weights[0].shape
    bias = math.log2(tgt_total) - lse[...]
    new[...] = square_norm(src[...]) + EPS * LN2 * bias
    base[...] = square_norm(tgt[...]) + EPS * math.log(src_total)
    top = jnp.max(bias, axis=1, keepdims=True)
    factors[...] = jnp.broadcast_to(jnp.exp2(bias - top), (8, n_src))

    for part in range(KEPT):
        total = jnp.zeros((share // 8, 8, 128), jnp.float32)
        for start in range(0, n_src, 128):
            powers = weights[part][:, start : start + 128].astype(jnp.float32).reshape(share // 8, 8, 128)
            total = total + powers * factors[:, start : start + 128][None]
        sums = total.reshape(share, 128).T.sum(0, keepdims=True)
        out[:, part * share : (part + 1) * share] = jnp.broadcast_to(sums, (out.shape[0], share))
    sums = out[...]
    good = jnp.logical_and(in_range(sums), jnp.min(bias) - jnp.max(bias) > -120.0)
    good = jnp.logical_and(good, flag[0, 0] == 1)
    out[...] = top - shift[...] + jnp.log2(sums)

    @pl.when(jnp.logical_not(good))
    def _():
        fill_streamed(src[...], bias, lhs)
        fill_fixed(tgt[...], rhs)
        exact_lse(lhs, rhs, out, 0.0)


ROW, X, Y, CORE = 8, 4, 4, 2


def from_row(v, k):
    return lax.ppermute(v, "row", [((z + k) % ROW, z) for z in range(ROW)])


def from_col(v, kx, ky, kc):
    pairs = []
    for x in range(X):
        for y in range(Y):
            for c in range(CORE):
                there = (((x + kx) % X) * Y + (y + ky) % Y) * CORE + (c + kc) % CORE
                pairs.append((there, (x * Y + y) * CORE + c))
    return lax.ppermute(v, "col", pairs)


def pair_lse(a, b):
    top = jnp.maximum(a, b)
    return top + jnp.log2(jnp.exp2(a - top) + jnp.exp2(b - top))


def ring_lse(own, others):
    top = jnp.maximum(jnp.maximum(others[0], others[2]), jnp.maximum(own, others[1]))
    near = jnp.exp2(others[0] - top) + jnp.exp2(others[2] - top)
    return top + jnp.log2(near + (jnp.exp2(own - top) + jnp.exp2(others[1] - top)))


def all_to_all(parts, axis):
    return lax.all_to_all(parts, axis, 0, 0, tiled=True)


def feature_order(per_src, per_tgt):
    col, row = lax.axis_index("col"), lax.axis_index("row")
    depth = per_src * X * Y * CORE
    at = lax.broadcasted_iota(jnp.int32, (depth, depth), 1)
    kx, ky, kc = (at // per_src) % X, (at // (per_src * X)) % Y, at // (per_src * X * Y)
    x, y, c = col // (Y * CORE), (col // CORE) % Y, col % CORE
    there = (((x + kx) % X) * Y + (y + ky) % Y) * CORE + (c + kc) % CORE
    src_feature = there * per_src + at % per_src
    at = lax.broadcasted_iota(jnp.int32, (depth, depth), 0)
    tgt_feature = at
    return (src_feature == tgt_feature).astype(jnp.bfloat16)


def on_device(source_points, target_points, target_potential):
    per_src, n_src = source_points.shape
    per_tgt, n_tgt = target_points.shape
    tgt_total = n_tgt * X * Y * CORE
    src_total = n_src * ROW
    dim = per_src * X * Y * CORE
    order = feature_order(per_src, per_tgt)

    src = source_points
    pot = target_potential.reshape(1, n_tgt)
    copies = jnp.broadcast_to(target_points[None], (ROW,) + target_points.shape)

    tgt = all_to_all(copies, "row")
    src = jnp.concatenate([src] + [from_col(source_points, k, 0, 0) for k in range(1, X)], axis=0)
    src = jnp.concatenate([src] + [from_col(src, 0, k, 0) for k in range(1, Y)], axis=0)
    far = from_col(src, 0, 0, 1)

    params = pltpu.CompilerParams(vmem_limit_bytes=12 * 2**20)
    f32, bf16 = jnp.float32, jnp.bfloat16
    whole, scalar = pl.BlockSpec(memory_space=pltpu.VMEM), pl.BlockSpec(memory_space=pltpu.SMEM)
    tgt = tgt.reshape(dim, n_tgt)
    *weights, lse, shift, flag, src = pl.pallas_call(
        first_kernel,
        out_shape=[
            *[pltpu.VMEM((n_tgt // KEPT, n_src), bf16)] * KEPT,
            jax.ShapeDtypeStruct((1, n_src), f32),
            jax.ShapeDtypeStruct((1, n_tgt), f32),
            jax.ShapeDtypeStruct((1, 1), jnp.int32),
            jax.ShapeDtypeStruct((dim, n_src), bf16),
        ],
        out_specs=[whole] * KEPT + [whole, whole, scalar, whole],
        scratch_shapes=[
            pltpu.VMEM((n_tgt, 4 * dim), bf16),
            pltpu.VMEM((4 * dim, n_src), bf16),
        ],
        compiler_params=params,
        name="first_pass",
    )(order, src, far, tgt, pot)

    lse = lse.reshape(n_src)
    lse = pair_lse(lse, from_col(lse, 0, 0, 1))
    lse = ring_lse(lse, [from_col(lse, k, 0, 0) for k in (1, 2, 3)])
    lse = ring_lse(lse, [from_col(lse, 0, k, 0) for k in (1, 2, 3)])

    source_new, base, parts = pl.pallas_call(
        functools.partial(second_kernel, tgt_total, src_total),
        out_shape=[
            jax.ShapeDtypeStruct((1, n_src), f32),
            jax.ShapeDtypeStruct((1, n_tgt), f32),
            jax.ShapeDtypeStruct((ROW, n_tgt), f32),
        ],
        in_specs=[whole, scalar, whole, whole, whole] + [whole] * KEPT,
        out_specs=[whole, whole, whole],
        scratch_shapes=[
            pltpu.VMEM((8, n_src), f32),
            pltpu.VMEM((n_src, 4 * dim), bf16),
            pltpu.VMEM((4 * dim, n_tgt), bf16),
        ],
        compiler_params=params,
        name="second_pass",
    )(lse.reshape(1, n_src), flag, shift, src, tgt, *weights)
    parts = all_to_all(parts.reshape(ROW, 1, n_tgt), "row")
    target_new = base.reshape(n_tgt) - EPS * LN2 * lse_of(parts).reshape(n_tgt)
    return source_new.reshape(n_src), target_new


def solution(mesh):
    return jax.shard_map(
        on_device,
        mesh=mesh,
        in_specs=(P("col", "row"), P("row", "col"), P("col")),
        out_specs=(P("row"), P("col")),
        check_vma=False,
    )
```

```python
import functools
import math

import jax
import jax.numpy as jnp
from jax import lax
from jax.experimental import pallas as pl
from jax.experimental.pallas import tpu as pltpu
from jax.sharding import PartitionSpec as P

EPS = 0.05
LN2 = math.log(2.0)
KAPPA = 1.0 / (EPS * LN2)
ROWS = 128
LANES = 4096
EXACT_LANES = 256
KEPT = 8
HEAD = 40.0


def split3(v):
    hi = v.astype(jnp.bfloat16)
    rest = v - hi.astype(jnp.float32)
    mid = rest.astype(jnp.bfloat16)
    low = (rest - mid.astype(jnp.float32)).astype(jnp.bfloat16)
    return hi, mid, low


def fill_streamed(points, bias, lhs):
    d, n = points.shape
    hi, mid, low = split3(bias)
    row = lax.broadcasted_iota(jnp.int32, (d, n), 0)
    rows = jnp.where(row == 0, hi.astype(jnp.float32), 0.0)
    rows = jnp.where(row == 1, mid.astype(jnp.float32), rows)
    rows = jnp.where(row == 2, low.astype(jnp.float32), rows)
    lhs[:, : 2 * d] = jnp.concatenate([points, rows.astype(jnp.bfloat16)], axis=0).T
    lhs[:, 2 * d :] = jnp.concatenate([points, points], axis=0).T


def fill_fixed(points, rhs):
    d, n = points.shape
    row = lax.broadcasted_iota(jnp.int32, (d, n), 0)
    hi, mid, low = split3(points.astype(jnp.float32) * (2.0 * KAPPA))
    rhs[:d] = hi
    rhs[d : 2 * d] = jnp.where(row < 3, 1.0, 0.0).astype(jnp.bfloat16)
    rhs[2 * d : 3 * d] = mid
    rhs[3 * d :] = low


def scores_of(lhs, start, weights):
    scores = jnp.dot(lhs[pl.ds(start, ROWS), :], weights, preferred_element_type=jnp.float32)
    return scores.reshape(ROWS // 8, 8, weights.shape[1])


def lanes_of(step, width):
    return pl.ds(pl.multiple_of(step * width, width), width)


def exact_lse(lhs, rhs, out, offset):
    def block(step, carry):
        lanes = lanes_of(step, EXACT_LANES)
        weights = rhs[:, lanes]

        def rows(k, state):
            peak, total = state
            scores = scores_of(lhs, pl.multiple_of(k * ROWS, ROWS), weights)
            new_peak = jnp.maximum(peak, scores.max(0))
            total = total * jnp.exp2(peak - new_peak) + jnp.exp2(scores - new_peak[None]).sum(0)
            return new_peak, total

        start = (jnp.full((8, EXACT_LANES), -jnp.inf, jnp.float32), jnp.zeros((8, EXACT_LANES), jnp.float32))
        peak, total = lax.fori_loop(0, lhs.shape[0] // ROWS, rows, start)
        top = peak.max(0, keepdims=True)
        lse = offset + top + jnp.log2((total * jnp.exp2(peak - top)).sum(0, keepdims=True))
        out[:, lanes] = jnp.broadcast_to(lse, (out.shape[0], EXACT_LANES))
        return carry

    lax.fori_loop(0, rhs.shape[1] // EXACT_LANES, block, 0)


def in_range(sums):
    return jnp.logical_and(jnp.min(sums) > 2.0**-90, jnp.max(sums) < 2.0**127)


def square_norm(points):
    return jnp.sum(jnp.square(points.astype(jnp.float32)), axis=0, keepdims=True)


def lse_of(parts):
    top = parts.max(0, keepdims=True)
    return top + jnp.log2(jnp.exp2(parts - top).sum(0, keepdims=True))


def first_kernel(order, near, far, tgt, pot, *refs):
    weights, (out, shift, flag, src, src_norm, tgt_norm, lhs, rhs) = refs[:KEPT], refs[KEPT:]
    share = weights[0].shape[0]
    features = jnp.concatenate([near[...], far[...]], axis=0)
    src[...] = jnp.dot(order[...], features, preferred_element_type=jnp.float32).astype(jnp.bfloat16)
    fill_fixed(src[...], rhs)
    src_norm[...] = square_norm(src[...])
    tgt_norm[...] = square_norm(tgt[...])
    bias = pot[...] - KAPPA * tgt_norm[...]
    offset = jnp.max(bias, axis=1, keepdims=True) - HEAD
    shift[...] = bias - offset
    fill_streamed(tgt[...], bias - offset, lhs)

    def block(step, carry):
        lanes = lanes_of(step, LANES)
        fixed = rhs[:, lanes]
        total = jnp.zeros((8, LANES), jnp.float32)
        for start in range(0, lhs.shape[0], ROWS):
            powers = jnp.exp2(scores_of(lhs, start, fixed))
            total = total + powers.sum(0)
            at = start % share
            weights[start // share][at : at + ROWS, lanes] = powers.reshape(ROWS, LANES).astype(jnp.bfloat16)
        out[:, lanes] = total.sum(0, keepdims=True)
        return carry

    lax.fori_loop(0, rhs.shape[1] // LANES, block, 0)
    sums = out[...]
    good = in_range(sums)
    flag[0, 0] = good.astype(jnp.int32)
    out[...] = offset + jnp.log2(sums)

    @pl.when(jnp.logical_not(good))
    def _():
        exact_lse(lhs, rhs, out, offset)


def second_kernel(tgt_total, lse, flag, shift, src, tgt, src_norm, *refs):
    weights, (new_out, out, factors, lhs, rhs, new, sem) = refs[:KEPT], refs[KEPT:]
    share, n_src = weights[0].shape
    bias = math.log2(tgt_total) - lse[...]
    new[...] = src_norm[...] + EPS * LN2 * bias
    leave = pltpu.make_async_copy(new, new_out, sem)
    leave.start()
    top = jnp.max(bias, axis=1, keepdims=True)
    factors[...] = jnp.broadcast_to(jnp.exp2(bias - top), (8, n_src))

    for part in range(KEPT):
        total = jnp.zeros((share // 8, 8, 128), jnp.float32)
        for start in range(0, n_src, 128):
            powers = weights[part][:, start : start + 128].astype(jnp.float32).reshape(share // 8, 8, 128)
            total = total + powers * factors[:, start : start + 128][None]
        sums = total.reshape(share, 128).T.sum(0, keepdims=True)
        out[:, part * share : (part + 1) * share] = jnp.broadcast_to(sums, (out.shape[0], share))
    sums = out[...]
    good = jnp.logical_and(in_range(sums), jnp.min(bias) - jnp.max(bias) > -120.0)
    good = jnp.logical_and(good, flag[0, 0] == 1)
    out[...] = top - shift[...] + jnp.log2(sums)

    @pl.when(jnp.logical_not(good))
    def _():
        fill_streamed(src[...], bias, lhs)
        fill_fixed(tgt[...], rhs)
        exact_lse(lhs, rhs, out, 0.0)

    leave.wait()


ROW, X, Y, CORE = 8, 4, 4, 2


def from_row(v, k):
    return lax.ppermute(v, "row", [((z + k) % ROW, z) for z in range(ROW)])


def from_col(v, kx, ky, kc):
    pairs = []
    for x in range(X):
        for y in range(Y):
            for c in range(CORE):
                there = (((x + kx) % X) * Y + (y + ky) % Y) * CORE + (c + kc) % CORE
                pairs.append((there, (x * Y + y) * CORE + c))
    return lax.ppermute(v, "col", pairs)


def pair_lse(a, b):
    top = jnp.maximum(a, b)
    return top + jnp.log2(jnp.exp2(a - top) + jnp.exp2(b - top))


def ring_lse(own, others):
    top = jnp.maximum(jnp.maximum(others[0], others[2]), jnp.maximum(own, others[1]))
    near = jnp.exp2(others[0] - top) + jnp.exp2(others[2] - top)
    return top + jnp.log2(near + (jnp.exp2(own - top) + jnp.exp2(others[1] - top)))


def all_to_all(parts, axis):
    return lax.all_to_all(parts, axis, 0, 0, tiled=True)


def feature_order(per_src, per_tgt):
    col, row = lax.axis_index("col"), lax.axis_index("row")
    depth = per_src * X * Y * CORE
    at = lax.broadcasted_iota(jnp.int32, (depth, depth), 1)
    kx, ky, kc = (at // per_src) % X, (at // (per_src * X)) % Y, at // (per_src * X * Y)
    x, y, c = col // (Y * CORE), (col // CORE) % Y, col % CORE
    there = (((x + kx) % X) * Y + (y + ky) % Y) * CORE + (c + kc) % CORE
    src_feature = there * per_src + at % per_src
    at = lax.broadcasted_iota(jnp.int32, (depth, depth), 0)
    tgt_feature = at
    return (src_feature == tgt_feature).astype(jnp.bfloat16)


def on_device(source_points, target_points, target_potential):
    per_src, n_src = source_points.shape
    per_tgt, n_tgt = target_points.shape
    tgt_total = n_tgt * X * Y * CORE
    src_total = n_src * ROW
    dim = per_src * X * Y * CORE
    order = feature_order(per_src, per_tgt)

    src = source_points
    pot = KAPPA * target_potential.reshape(1, n_tgt)
    copies = jnp.broadcast_to(target_points[None], (ROW,) + target_points.shape)

    tgt = all_to_all(copies, "row")
    src = jnp.concatenate([src] + [from_col(source_points, k, 0, 0) for k in range(1, X)], axis=0)
    src = jnp.concatenate([src] + [from_col(src, 0, k, 0) for k in range(1, Y)], axis=0)
    far = from_col(src, 0, 0, 1)

    params = pltpu.CompilerParams(vmem_limit_bytes=12 * 2**20)
    f32, bf16 = jnp.float32, jnp.bfloat16
    whole, scalar = pl.BlockSpec(memory_space=pltpu.VMEM), pl.BlockSpec(memory_space=pltpu.SMEM)
    tgt = tgt.reshape(dim, n_tgt)
    *weights, lse, shift, flag, src, src_norm, tgt_norm = pl.pallas_call(
        first_kernel,
        out_shape=[
            *[pltpu.VMEM((n_tgt // KEPT, n_src), bf16)] * KEPT,
            jax.ShapeDtypeStruct((1, n_src), f32),
            jax.ShapeDtypeStruct((1, n_tgt), f32),
            jax.ShapeDtypeStruct((1, 1), jnp.int32),
            jax.ShapeDtypeStruct((dim, n_src), bf16),
            jax.ShapeDtypeStruct((1, n_src), f32),
            jax.ShapeDtypeStruct((1, n_tgt), f32),
        ],
        out_specs=[whole] * KEPT + [whole, whole, scalar, whole, whole, whole],
        scratch_shapes=[
            pltpu.VMEM((n_tgt, 4 * dim), bf16),
            pltpu.VMEM((4 * dim, n_src), bf16),
        ],
        compiler_params=params,
        name="first_pass",
    )(order, src, far, tgt, pot)

    lse = lse.reshape(n_src)
    lse = pair_lse(lse, from_col(lse, 0, 0, 1))
    lse = ring_lse(lse, [from_col(lse, k, 0, 0) for k in (1, 2, 3)])
    lse = ring_lse(lse, [from_col(lse, 0, k, 0) for k in (1, 2, 3)])

    source_new, parts = pl.pallas_call(
        functools.partial(second_kernel, tgt_total),
        out_shape=[jax.ShapeDtypeStruct((1, n_src), f32), jax.ShapeDtypeStruct((ROW, n_tgt), f32)],
        in_specs=[whole, scalar, whole, whole, whole, whole] + [whole] * KEPT,
        out_specs=[pl.BlockSpec(memory_space=pl.ANY), whole],
        scratch_shapes=[
            pltpu.VMEM((8, n_src), f32),
            pltpu.VMEM((n_src, 4 * dim), bf16),
            pltpu.VMEM((4 * dim, n_tgt), bf16),
            pltpu.VMEM((1, n_src), f32),
            pltpu.SemaphoreType.DMA,
        ],
        compiler_params=params,
        name="second_pass",
    )(lse.reshape(1, n_src), flag, shift, src, tgt, src_norm, *weights)
    parts = all_to_all(parts.reshape(ROW, 1, n_tgt), "row")
    target_new = tgt_norm.reshape(n_tgt) - EPS * LN2 * lse_of(parts).reshape(n_tgt) + EPS * math.log(src_total)
    return source_new.reshape(n_src), target_new


def solution(mesh):
    return jax.shard_map(
        on_device,
        mesh=mesh,
        in_specs=(P("col", "row"), P("row", "col"), P("col")),
        out_specs=(P("row"), P("col")),
        check_vma=False,
    )
```

```python
import functools
import math

import jax
import jax.numpy as jnp
from jax import lax
from jax.experimental import pallas as pl
from jax.experimental.pallas import tpu as pltpu
from jax.sharding import PartitionSpec as P

EPS = 0.05
LN2 = math.log(2.0)
KAPPA = 1.0 / (EPS * LN2)
ROWS = 128
LANES = 4096
EXACT_LANES = 256
KEPT = 8
HEAD = 40.0


def split3(v):
    hi = v.astype(jnp.bfloat16)
    rest = v - hi.astype(jnp.float32)
    mid = rest.astype(jnp.bfloat16)
    low = (rest - mid.astype(jnp.float32)).astype(jnp.bfloat16)
    return hi, mid, low


def fill_streamed(points, bias, lhs):
    d, n = points.shape
    hi, mid, low = split3(bias)
    row = lax.broadcasted_iota(jnp.int32, (d, n), 0)
    rows = jnp.where(row == 0, hi.astype(jnp.float32), 0.0)
    rows = jnp.where(row == 1, mid.astype(jnp.float32), rows)
    rows = jnp.where(row == 2, low.astype(jnp.float32), rows)
    lhs[:, : 2 * d] = jnp.concatenate([points, rows.astype(jnp.bfloat16)], axis=0).T
    lhs[:, 2 * d :] = jnp.concatenate([points, points], axis=0).T


def fill_fixed(points, rhs):
    d, n = points.shape
    row = lax.broadcasted_iota(jnp.int32, (d, n), 0)
    hi, mid, low = split3(points.astype(jnp.float32) * (2.0 * KAPPA))
    rhs[:d] = hi
    rhs[d : 2 * d] = jnp.where(row < 3, 1.0, 0.0).astype(jnp.bfloat16)
    rhs[2 * d : 3 * d] = mid
    rhs[3 * d :] = low


def scores_of(lhs, start, weights):
    scores = jnp.dot(lhs[pl.ds(start, ROWS), :], weights, preferred_element_type=jnp.float32)
    return scores.reshape(ROWS // 8, 8, weights.shape[1])


def lanes_of(step, width):
    return pl.ds(pl.multiple_of(step * width, width), width)


def exact_lse(lhs, rhs, out, offset):
    def block(step, carry):
        lanes = lanes_of(step, EXACT_LANES)
        weights = rhs[:, lanes]

        def rows(k, state):
            peak, total = state
            scores = scores_of(lhs, pl.multiple_of(k * ROWS, ROWS), weights)
            new_peak = jnp.maximum(peak, scores.max(0))
            total = total * jnp.exp2(peak - new_peak) + jnp.exp2(scores - new_peak[None]).sum(0)
            return new_peak, total

        start = (jnp.full((8, EXACT_LANES), -jnp.inf, jnp.float32), jnp.zeros((8, EXACT_LANES), jnp.float32))
        peak, total = lax.fori_loop(0, lhs.shape[0] // ROWS, rows, start)
        top = peak.max(0, keepdims=True)
        lse = offset + top + jnp.log2((total * jnp.exp2(peak - top)).sum(0, keepdims=True))
        out[:, lanes] = jnp.broadcast_to(lse, (out.shape[0], EXACT_LANES))
        return carry

    lax.fori_loop(0, rhs.shape[1] // EXACT_LANES, block, 0)


def in_range(sums):
    return jnp.logical_and(jnp.min(sums) > 2.0**-90, jnp.max(sums) < 2.0**127)


def square_norm(points):
    return jnp.sum(jnp.square(points.astype(jnp.float32)), axis=0, keepdims=True)


def first_kernel(order, near, far, tgt, pot, *refs):
    weights, (out, shift, flag, src, src_norm, tgt_norm, lhs, rhs) = refs[:KEPT], refs[KEPT:]
    share = weights[0].shape[0]
    features = jnp.concatenate([near[...], far[...]], axis=0)
    src[...] = jnp.dot(order[...], features, preferred_element_type=jnp.float32).astype(jnp.bfloat16)
    fill_fixed(src[...], rhs)
    src_norm[...] = square_norm(src[...])
    tgt_norm[...] = square_norm(tgt[...])
    bias = pot[...] - KAPPA * tgt_norm[...]
    offset = jnp.max(bias, axis=1, keepdims=True) - HEAD
    shift[...] = bias - offset
    fill_streamed(tgt[...], bias - offset, lhs)

    def block(step, carry):
        lanes = lanes_of(step, LANES)
        fixed = rhs[:, lanes]
        total = jnp.zeros((8, LANES), jnp.float32)
        for start in range(0, lhs.shape[0], ROWS):
            powers = jnp.exp2(scores_of(lhs, start, fixed))
            total = total + powers.sum(0)
            at = start % share
            weights[start // share][at : at + ROWS, lanes] = powers.reshape(ROWS, LANES).astype(jnp.bfloat16)
        out[:, lanes] = total.sum(0, keepdims=True)
        return carry

    lax.fori_loop(0, rhs.shape[1] // LANES, block, 0)
    sums = out[...]
    good = in_range(sums)
    flag[0, 0] = good.astype(jnp.int32)
    out[...] = offset + jnp.log2(sums)

    @pl.when(jnp.logical_not(good))
    def _():
        exact_lse(lhs, rhs, out, offset)


def second_kernel(tgt_total, lse, flag, shift, src, tgt, src_norm, *refs):
    weights, (new_out, out, factors, lhs, rhs, new, sem) = refs[:KEPT], refs[KEPT:]
    share, n_src = weights[0].shape
    bias = math.log2(tgt_total) - lse[...]
    new[...] = src_norm[...] + EPS * LN2 * bias
    leave = pltpu.make_async_copy(new, new_out, sem)
    leave.start()
    top = jnp.max(bias, axis=1, keepdims=True)
    factors[...] = jnp.broadcast_to(jnp.exp2(bias - top), (8, n_src))

    for part in range(KEPT):
        total = jnp.zeros((share // 8, 8, 128), jnp.float32)
        for start in range(0, n_src, 128):
            powers = weights[part][:, start : start + 128].astype(jnp.float32).reshape(share // 8, 8, 128)
            total = total + powers * factors[:, start : start + 128][None]
        sums = total.reshape(share, 128).T.sum(0, keepdims=True)
        out[:, part * share : (part + 1) * share] = jnp.broadcast_to(sums, (out.shape[0], share))
    sums = out[...]
    good = jnp.logical_and(in_range(sums), jnp.min(bias) - jnp.max(bias) > -120.0)
    good = jnp.logical_and(good, flag[0, 0] == 1)
    out[...] = top - shift[...] + jnp.log2(sums)

    @pl.when(jnp.logical_not(good))
    def _():
        fill_streamed(src[...], bias, lhs)
        fill_fixed(tgt[...], rhs)
        exact_lse(lhs, rhs, out, 0.0)

    leave.wait()


ROW, X, Y, CORE = 8, 4, 4, 2


def from_row(v, k):
    return lax.ppermute(v, "row", [((z + k) % ROW, z) for z in range(ROW)])


def from_col(v, kx, ky, kc):
    pairs = []
    for x in range(X):
        for y in range(Y):
            for c in range(CORE):
                there = (((x + kx) % X) * Y + (y + ky) % Y) * CORE + (c + kc) % CORE
                pairs.append((there, (x * Y + y) * CORE + c))
    return lax.ppermute(v, "col", pairs)


def lse_of_rows(parts):
    rows = [parts[k] for k in range(ROW)]
    top = functools.reduce(jnp.maximum, rows)
    return top + jnp.log2(functools.reduce(jnp.add, [jnp.exp2(row - top) for row in rows]))


def pair_lse(a, b):
    top = jnp.maximum(a, b)
    return top + jnp.log2(jnp.exp2(a - top) + jnp.exp2(b - top))


def ring_lse(own, others):
    top = jnp.maximum(jnp.maximum(others[0], others[2]), jnp.maximum(own, others[1]))
    near = jnp.exp2(others[0] - top) + jnp.exp2(others[2] - top)
    return top + jnp.log2(near + (jnp.exp2(own - top) + jnp.exp2(others[1] - top)))


def all_to_all(parts, axis):
    return lax.all_to_all(parts, axis, 0, 0, tiled=True)


def feature_order(per_src, per_tgt):
    col, row = lax.axis_index("col"), lax.axis_index("row")
    depth = per_src * X * Y * CORE
    at = lax.broadcasted_iota(jnp.int32, (depth, depth), 1)
    kx, ky, kc = (at // per_src) % X, (at // (per_src * X)) % Y, at // (per_src * X * Y)
    x, y, c = col // (Y * CORE), (col // CORE) % Y, col % CORE
    there = (((x + kx) % X) * Y + (y + ky) % Y) * CORE + (c + kc) % CORE
    src_feature = there * per_src + at % per_src
    at = lax.broadcasted_iota(jnp.int32, (depth, depth), 0)
    tgt_feature = at
    return (src_feature == tgt_feature).astype(jnp.bfloat16)


def on_device(source_points, target_points, target_potential):
    per_src, n_src = source_points.shape
    per_tgt, n_tgt = target_points.shape
    tgt_total = n_tgt * X * Y * CORE
    src_total = n_src * ROW
    dim = per_src * X * Y * CORE
    order = feature_order(per_src, per_tgt)

    src = source_points
    pot = KAPPA * target_potential.reshape(1, n_tgt)
    copies = jnp.broadcast_to(target_points[None], (ROW,) + target_points.shape)

    tgt = all_to_all(copies, "row")
    src = jnp.concatenate([src] + [from_col(source_points, k, 0, 0) for k in range(1, X)], axis=0)
    src = jnp.concatenate([src] + [from_col(src, 0, k, 0) for k in range(1, Y)], axis=0)
    far = from_col(src, 0, 0, 1)

    params = pltpu.CompilerParams(vmem_limit_bytes=12 * 2**20)
    f32, bf16 = jnp.float32, jnp.bfloat16
    whole, scalar = pl.BlockSpec(memory_space=pltpu.VMEM), pl.BlockSpec(memory_space=pltpu.SMEM)
    tgt = tgt.reshape(dim, n_tgt)
    *weights, lse, shift, flag, src, src_norm, tgt_norm = pl.pallas_call(
        first_kernel,
        out_shape=[
            *[pltpu.VMEM((n_tgt // KEPT, n_src), bf16)] * KEPT,
            jax.ShapeDtypeStruct((1, n_src), f32),
            jax.ShapeDtypeStruct((1, n_tgt), f32),
            jax.ShapeDtypeStruct((1, 1), jnp.int32),
            jax.ShapeDtypeStruct((dim, n_src), bf16),
            jax.ShapeDtypeStruct((1, n_src), f32),
            jax.ShapeDtypeStruct((1, n_tgt), f32),
        ],
        out_specs=[whole] * KEPT + [whole, whole, scalar, whole, whole, whole],
        scratch_shapes=[
            pltpu.VMEM((n_tgt, 4 * dim), bf16),
            pltpu.VMEM((4 * dim, n_src), bf16),
        ],
        compiler_params=params,
        name="first_pass",
    )(order, src, far, tgt, pot)

    lse = lse.reshape(n_src)
    lse = pair_lse(lse, from_col(lse, 0, 0, 1))
    lse = ring_lse(lse, [from_col(lse, k, 0, 0) for k in (1, 2, 3)])
    lse = ring_lse(lse, [from_col(lse, 0, k, 0) for k in (1, 2, 3)])

    source_new, parts = pl.pallas_call(
        functools.partial(second_kernel, tgt_total),
        out_shape=[jax.ShapeDtypeStruct((1, n_src), f32), jax.ShapeDtypeStruct((ROW, n_tgt), f32)],
        in_specs=[whole, scalar, whole, whole, whole, whole] + [whole] * KEPT,
        out_specs=[pl.BlockSpec(memory_space=pl.ANY), whole],
        scratch_shapes=[
            pltpu.VMEM((8, n_src), f32),
            pltpu.VMEM((n_src, 4 * dim), bf16),
            pltpu.VMEM((4 * dim, n_tgt), bf16),
            pltpu.VMEM((1, n_src), f32),
            pltpu.SemaphoreType.DMA,
        ],
        compiler_params=params,
        name="second_pass",
    )(lse.reshape(1, n_src), flag, shift, src, tgt, src_norm, *weights)
    parts = all_to_all(parts.reshape(ROW, 1, n_tgt), "row")
    target_new = tgt_norm.reshape(n_tgt) - EPS * LN2 * lse_of_rows(parts.reshape(ROW, n_tgt)) + EPS * math.log(src_total)
    return source_new.reshape(n_src), target_new


def solution(mesh):
    return jax.shard_map(
        on_device,
        mesh=mesh,
        in_specs=(P("col", "row"), P("row", "col"), P("col")),
        out_specs=(P("row"), P("col")),
        check_vma=False,
    )
```
